32 devices in a mesh: dp: 8 (over z, y), tensor: 4 (over x, core).
Axes of the slice: x: 2, y: 2, z: 4, core: 2. Of those that a mesh axis runs over, the one named last changes fastest.
Arguments:
- cotangent: bfloat16 [1024, 4096], P('dp', 'tensor'), may hold values from -6 to 6
- gate_pre: bfloat16 [1024, 14336], P('dp', 'tensor'), may hold values from -6 to 6
- up_pre: bfloat16 [1024, 14336], P('dp', 'tensor'), may hold values from -6 to 6
- down_weight: bfloat16 [14336, 4096], P('tensor', 'dp'), may hold values from -0.046875 to 0.046875
Outputs:
- grad_gate: bfloat16 [1024, 14336], P('dp', 'tensor')
- grad_up: bfloat16 [1024, 14336], P('dp', 'tensor')
- grad_down: float32 [14336, 4096], P('tensor', 'dp')
The draws below stay inside these ranges and needn't reach their ends.
All inputs are finite; a program needn't handle non-finite values.
Results may differ from the reference program's by a relative error of at most 0.003.
Values may be sent and summed in bfloat16 or wider, within the bound.
No kernel may reach another device: no remote copies, remote signals or barrier semaphores. Data moves between devices by JAX's collectives and lax.ppermute only.
A program may use at most 128 MiB of HBM per device.

```python
import jax
import jax.numpy as jnp

D = 4096
FF = 14336
TOKENS = 1024


def with_spikes(drawn, key, source, target, shards_of, factor):
    owner, partner = [(jnp.arange(drawn.shape[axis_at]) // (drawn.shape[axis_at] // shards_of)).reshape([-1 if axis == axis_at else 1 for axis in range(drawn.ndim)]) for axis_at in (source, target)]
    chosen = jax.random.permutation(key, shards_of)[partner]
    strong = (owner == chosen) | (owner == (partner + shards_of // 2) % shards_of)
    return jnp.where(strong, factor * drawn, drawn)


def steps_of(own_key, extent, shards, least, top_value):
    def one(position, parts):
        steps = jax.random.uniform(jax.random.fold_in(jax.random.fold_in(own_key, 6), position), (parts,), jnp.float32, least / len(shards), top_value / len(shards))
        return jnp.repeat(jnp.exp(steps), extent[position] // parts).reshape((-1,) + (1,) * (len(extent) - position - 1))

    gain = one(*shards[0])
    for cut in shards[1:]:
        gain = gain * one(*cut)
    return gain


def noise(own_key, extent, spread, reach, pieces=(), held_as=jnp.bfloat16):
    result = spread * jax.random.normal(own_key, extent, jnp.float32)
    if pieces:
        result = result * steps_of(own_key, extent, pieces, -0.22, 0.18)
    return jnp.clip(result, -reach, reach).astype(held_as)


def bell_draw_with(key, shape, scale, reach, split, heavy, held_as=jnp.bfloat16):
    drawn = scale * jax.random.normal(key, shape, jnp.float32)
    if split:
        drawn = drawn * steps_of(key, shape, split, -0.22, 0.18)
    return jnp.clip(with_spikes(drawn, jax.random.fold_in(key, 3), *heavy), -reach, reach).astype(held_as)


def setup_inputs(seed: int = 0) -> dict:
    key_of = jax.random.split(jax.random.key(seed), 5)
    cotangent = bell_draw_with(key_of[0], (TOKENS, D), 1.0, 6.0, ((0, 8), (1, 4)), (0, 1, 8, 2.0))
    gate_pre = noise(key_of[1], (TOKENS, FF), 1.0, 6.0, ((0, 8), (1, 4)))
    up_pre = noise(key_of[2], (TOKENS, FF), 1.0, 6.0, ((0, 8), (1, 4)))
    down_weight = noise(key_of[3], (FF, D), FF ** -0.5, 0.046875, ((0, 4), (1, 8)))
    return dict(cotangent=cotangent, gate_pre=gate_pre, up_pre=up_pre, down_weight=down_weight)


def reference(cotangent, gate_pre, up_pre, down_weight):
    gate_vals = gate_pre.astype(jnp.float32)
    up_vals = up_pre.astype(jnp.float32)
    sigma = jax.nn.sigmoid(gate_vals)
    act_vals = gate_vals * sigma
    hidden = (act_vals * up_vals).astype(jnp.bfloat16)
    dhid = jnp.dot(cotangent, down_weight.T, preferred_element_type=jnp.float32)
    grad_up = (dhid * act_vals).astype(jnp.bfloat16)
    grad_gate = (dhid * up_vals * sigma * (1.0 + gate_vals * (1.0 - sigma))).astype(jnp.bfloat16)
    grad_down = jnp.dot(hidden.T, cotangent, preferred_element_type=jnp.float32) * (TOKENS ** -0.5)
    return grad_gate, grad_up, grad_down
```

```python
import jax
import jax.numpy as jnp
from jax import lax
from jax.sharding import PartitionSpec as P

WIRE = jnp.float16
WIRE_SCALE = 16.0


def after(value, *others):
    return lax.optimization_barrier((value,) + others)[0]


def shards(cotangent, gate_pre, up_pre, down_weight):
    dp, tensor = lax.axis_size("dp"), lax.axis_size("tensor")
    line = dp // 2
    tokens, features = cotangent.shape
    hidden_units, half = down_weight.shape
    assert features == 2 * half and line == tensor and line % 2 == 0
    position, side = lax.axis_index("dp") // 2, lax.axis_index("dp") % 2
    shard = lax.axis_index("tensor")
    columns = hidden_units * 4 // 7

    def along(name, value, step, first, last):
        pairs = [(2 * at + s, 2 * (at + step) + s) for at in range(first, last + 1) for s in (0, 1)]
        with jax.named_scope(name):
            return lax.ppermute(value, "dp", pairs)

    def across(name, value):
        with jax.named_scope(name):
            return lax.ppermute(value, "dp", [(at, at ^ 1) for at in range(dp)])

    gate_vals = gate_pre.astype(jnp.float32)
    up_vals = up_pre.astype(jnp.float32)
    sigma = jax.nn.sigmoid(gate_vals)
    act_vals = gate_vals * sigma
    hidden = (act_vals * up_vals).astype(jnp.bfloat16)
    first, last = hidden[:, :columns], hidden[:, columns:]
    weight_first, weight_last = down_weight[:columns], down_weight[columns:]

    last_other = across("hidden_last_side", last)
    first_up = along("hidden_first_up1", first, 1, 0, line - 2)
    first_down = along("hidden_first_down1", first, -1, 1, line - 1)
    weight_other = across("weight_side", weight_first)

    block = after(cotangent, hidden)
    arrived = []
    for turn in range(tensor // 2):
        pairs = [
            ((2 * at + s) * tensor + owner, (2 * owner + s) * tensor + (at + 2 * turn) % tensor)
            for at in range(line)
            for s in (0, 1)
            for owner in range(tensor)
        ]
        with jax.named_scope("cotangent_spread"):
            arrived.append(lax.ppermute(block, ("dp", "tensor"), pairs))
    odd = (position - shard) % 2
    turned = ((shard - position + odd) % line) // 2
    row = lax.dynamic_slice_in_dim(jnp.stack(arrived + arrived), turned, line // 2, 0)
    mine = jnp.where(side == 0, row[..., :half], row[..., half:])
    other = jnp.where(side == 0, row[..., half:], row[..., :half])
    theirs = across("cotangent_side", after(other, last_other))

    both_last = jnp.stack([last, last_other])
    last_up = along("hidden_last_up1", both_last, 1, 0, line - 2)
    last_down = along("hidden_last_down1", both_last, -1, 1, line - 1)

    own = jnp.stack([mine, other, theirs])
    with jax.named_scope("cotangent_core"):
        swapped = lax.ppermute(
            after(own, first_up, first_down), "tensor", [(at, at ^ 1) for at in range(tensor)]
        )
    whole = jnp.stack([jnp.where(odd == 0, own, swapped), jnp.where(odd == 0, swapped, own)], axis=2)
    mine, other, theirs = whole.reshape(3, line, tokens, half)
    features_of_all = jnp.stack([mine, theirs], axis=1)

    def product(left, right):
        return jnp.einsum("...f,hf->...h", left, right, preferred_element_type=jnp.float32)

    parts = {"last": product(features_of_all, weight_last) * WIRE_SCALE}
    parts["first"] = (product(mine, weight_first) + product(other, weight_other)) * WIRE_SCALE

    rising = {"first": [first, first_up], "last": [both_last, last_up]}
    falling = {"first": [first, first_down], "last": [both_last, last_down]}
    up_sum = {"first": 0.0, "last": 0.0}
    down_sum = {"first": 0.0, "last": 0.0}
    sides = {}
    steps = [(first_up, first_down), (last_up, last_down)]

    def gather_step(which, step, waits):
        up = along(f"hidden_{which}_up{step}", after(rising[which][-1], *waits), 1, step - 1, line - 2)
        down = along(f"hidden_{which}_down{step}", after(falling[which][-1], *waits), -1, 1, line - step)
        rising[which].append(up)
        falling[which].append(down)
        return up, down

    def sum_step(which, step, waits):
        message = after((parts[which][step] + up_sum[which]).astype(WIRE), *waits)
        up = along(f"dhid_{which}_up{step}", message, 1, 0, step - 1)
        message = after((parts[which][line - step] + down_sum[which]).astype(WIRE), *waits)
        down = along(f"dhid_{which}_down{step}", message, -1, line - step, line - 1)
        up_sum[which], down_sum[which] = up.astype(jnp.float32), down.astype(jnp.float32)
        return up, down

    def gathered(which, k):
        if k == 0:
            return rising[which][0]
        return jnp.where(position >= k, rising[which][k], falling[which][line - k])

    def exchange(*ks):
        blocks = jnp.stack([gathered("first", k) for k in ks])
        swapped = across("hidden_first_side", after(blocks, weight_other))
        for n, k in enumerate(ks):
            sides[k] = blocks[n], swapped[n]
        return (swapped,)

    for step in range(1, line):
        for which, summed in (("first", "last"), ("last", "first")):
            waits, ended = steps[-2], ()
            if step + 1 < line:
                ended += gather_step(which, step + 1, waits)
            ended += sum_step(summed, step, waits)
            if which == "last":
                ready = [k for k in range(line) if max(k, line - k if k else 1) == step]
                if ready:
                    ended += exchange(*ready)
            steps.append(ended)

    def total(which):
        return parts[which][0] + up_sum[which] + down_sum[which]

    pair = total("last")
    dhid_last = pair[0] + across("dhid_last_side", pair[1].astype(WIRE)).astype(jnp.float32)
    dhid = jnp.concatenate([total("first"), dhid_last], axis=1) * (1.0 / WIRE_SCALE)

    grad_up = (dhid * act_vals).astype(jnp.bfloat16)
    grad_gate = (dhid * up_vals * sigma * (1.0 + gate_vals * (1.0 - sigma))).astype(jnp.bfloat16)

    hidden_first = jnp.stack([jnp.stack(sides[k]) for k in range(line)])
    hidden_last = jnp.stack([gathered("last", k) for k in range(line)])

    def weight_grad(values):
        return jnp.einsum("kstc,kstf->cf", values, features_of_all, preferred_element_type=jnp.float32)

    grad_down = jnp.concatenate([weight_grad(hidden_first), weight_grad(hidden_last)]) * (tokens * dp) ** (-0.5)
    return grad_gate, grad_up, grad_down


def solution(mesh):
    in_specs = (P("dp", "tensor"), P("dp", "tensor"), P("dp", "tensor"), P("tensor", "dp"))
    out_specs = (P("dp", "tensor"), P("dp", "tensor"), P("tensor", "dp"))
    return jax.shard_map(shards, mesh=mesh, in_specs=in_specs, out_specs=out_specs, check_vma=False)
```

```python
import jax
import jax.numpy as jnp
from jax import lax
from jax.sharding import PartitionSpec as P

WIRE = jnp.float16
WIRE_SCALE = 16.0


def after(value, *others):
    return lax.optimization_barrier((value,) + others)[0]


def together(*values):
    return list(lax.optimization_barrier(values))


def shards(cotangent, gate_pre, up_pre, down_weight):
    dp, tensor = lax.axis_size("dp"), lax.axis_size("tensor")
    line = dp // 2
    tokens, features = cotangent.shape
    hidden_units, half = down_weight.shape
    assert features == 2 * half and line == tensor and line % 2 == 0
    position, side = lax.axis_index("dp") // 2, lax.axis_index("dp") % 2
    shard = lax.axis_index("tensor")
    columns = hidden_units * 4 // 7

    def along(name, value, step, first, last):
        pairs = [(2 * at + s, 2 * (at + step) + s) for at in range(first, last + 1) for s in (0, 1)]
        with jax.named_scope(name):
            return lax.ppermute(value, "dp", pairs)

    def across(name, value):
        with jax.named_scope(name):
            return lax.ppermute(value, "dp", [(at, at ^ 1) for at in range(dp)])

    gate_vals = gate_pre.astype(jnp.float32)
    up_vals = up_pre.astype(jnp.float32)
    sigma = jax.nn.sigmoid(gate_vals)
    act_vals = gate_vals * sigma
    hidden = (act_vals * up_vals).astype(jnp.bfloat16)
    first, last = hidden[:, :columns], hidden[:, columns:]
    weight_first, weight_last = down_weight[:columns], down_weight[columns:]

    middle = columns // 4
    weight_other = [across("weight_side", weight_first[:middle])]

    share = 2 * tokens // tensor
    arrived = []
    for turn in range(tensor // 2):
        piece = lax.dynamic_slice_in_dim(cotangent, (position + 2 * turn) % tensor // 2 * share, share, 0)
        pairs = [
            ((2 * at + s) * tensor + owner, (2 * owner + s) * tensor + (at + 2 * turn) % tensor)
            for at in range(line)
            for s in (0, 1)
            for owner in range(tensor)
        ]
        with jax.named_scope("cotangent_spread"):
            arrived.append(lax.ppermute(piece, ("dp", "tensor"), pairs))
    odd = (position - shard) % 2
    turned = ((shard - position + odd) % line) // 2
    row = lax.dynamic_slice_in_dim(jnp.stack(arrived + arrived), turned, line // 2, 0)
    mine = jnp.where(side == 0, row[..., :half], row[..., half:])
    other = jnp.where(side == 0, row[..., half:], row[..., :half])

    last_other = across("hidden_last_side", last)
    first_sent = after(first, *arrived)
    first_up = along("hidden_first_up1", first_sent, 1, 0, line - 2)
    first_down = along("hidden_first_down1", first_sent, -1, 1, line - 1)
    theirs = across("cotangent_side", after(other, last_other))
    first_up, first_down = together(first_up, first_down)

    both_last = jnp.stack([last, last_other])
    last_up = along("hidden_last_up1", both_last, 1, 0, line - 2)
    last_down = along("hidden_last_down1", both_last, -1, 1, line - 1)
    weight_other.append(across("weight_side", after(weight_first[middle:], theirs)))
    last_up, last_down = together(last_up, last_down)

    own = after(jnp.stack([mine, other, theirs])[:, :, None], weight_other[0])
    bit = tensor // 2
    while bit > 1:
        with jax.named_scope("cotangent_shares"):
            swapped = lax.ppermute(own, "tensor", [(at, at ^ bit) for at in range(tensor)])
        low = (shard // bit) % 2 == 0
        own = jnp.stack([jnp.where(low, own, swapped), jnp.where(low, swapped, own)], axis=3)
        own = own.reshape(3, line // 2, -1, share, half)
        bit //= 2
    own = after(own, first_up)
    with jax.named_scope("cotangent_core"):
        swapped = lax.ppermute(own, "tensor", [(at, at ^ 1) for at in range(tensor)])
    whole = jnp.stack([jnp.where(odd == 0, own, swapped), jnp.where(odd == 0, swapped, own)], axis=2)
    mine, other, theirs = whole.reshape(3, line, tokens, half)
    features_of_all = jnp.stack([mine, theirs], axis=1)

    def product(left, right):
        return jnp.einsum("...f,hf->...h", left, right, preferred_element_type=jnp.float32)

    parts = {"last": product(features_of_all, weight_last) * WIRE_SCALE}

    rising = {"first": [first, first_up], "last": [both_last, last_up]}
    falling = {"first": [first, first_down], "last": [both_last, last_down]}
    up_sum = {"first": 0.0, "last": 0.0}
    down_sum = {"first": 0.0, "last": 0.0}
    sides = {}

    def gather_step(which, step, waits):
        up = along(f"hidden_{which}_up{step}", after(rising[which][-1], *waits), 1, step - 1, line - 2)
        down = along(f"hidden_{which}_down{step}", after(falling[which][-1], *waits), -1, 1, line - step)
        return [up, down]

    def sum_step(which, step, waits):
        message = after((parts[which][step] + up_sum[which]).astype(WIRE), *waits)
        up = along(f"dhid_{which}_up{step}", message, 1, 0, step - 1)
        message = after((parts[which][line - step] + down_sum[which]).astype(WIRE), *waits)
        down = along(f"dhid_{which}_down{step}", message, -1, line - step, line - 1)
        return [up, down]

    def gathered(which, k):
        if k == 0:
            return rising[which][0]
        return jnp.where(position >= k, rising[which][k], falling[which][line - k])

    def exchange(k, waits):
        block = gathered("first", k)
        return block, across("hidden_first_side", after(block, *waits))

    rounds = [first_up, last_up]
    waiting, sent = [0], []
    for step in range(1, line):
        for which, summed in (("first", "last"), ("last", "first")):
            begin = step == 1 and which == "first"
            if step == 1 and summed == "first":
                weight_other = jnp.concatenate(weight_other)
                parts["first"] = (product(mine, weight_first) + product(other, weight_other)) * WIRE_SCALE
            moved = sum_step(summed, step, rounds[-2:-1])
            if step + 1 < line:
                moved += gather_step(which, step + 1, rounds[-2:-1])
            ahead = []
            if not begin:
                ahead = [(k,) + exchange(k, rounds[-2:-1]) for k in waiting]
                waiting = []
            if begin:
                moved.append(weight_other[1])
            moved = together(*moved, *[swapped for _, _, swapped in sent])
            for k, block, _ in reversed(sent):
                sides[k] = block, moved.pop()
            if begin:
                weight_other[1] = moved.pop()
            if step + 1 < line:
                falling[which].append(moved.pop())
                rising[which].append(moved.pop())
                if which == "first":
                    waiting = waiting + [k for k in range(1, line) if max(k, line - k) == step + 1]
            sent = ahead
            up_sum[summed], down_sum[summed] = (value.astype(jnp.float32) for value in moved)
            rounds.append(moved[0])
    for k, *blocks in sent:
        sides[k] = blocks

    def total(which):
        return parts[which][0] + up_sum[which] + down_sum[which]

    pair = total("last")
    dhid_last = pair[0] + across("dhid_last_side", pair[1].astype(WIRE)).astype(jnp.float32)
    dhid = jnp.concatenate([total("first"), dhid_last], axis=1) * (1.0 / WIRE_SCALE)

    grad_up = (dhid * act_vals).astype(jnp.bfloat16)
    grad_gate = (dhid * up_vals * sigma * (1.0 + gate_vals * (1.0 - sigma))).astype(jnp.bfloat16)

    hidden_first = jnp.stack([jnp.stack(sides[k]) for k in range(line)])
    hidden_last = jnp.stack([gathered("last", k) for k in range(line)])

    def weight_grad(values):
        summed = jnp.einsum("kstc,kstf->cf", values, features_of_all, preferred_element_type=jnp.float32)
        return summed * (tokens * dp) ** (-0.5)

    grad_down = jnp.zeros(down_weight.shape, jnp.float32)
    grad_down = lax.dynamic_update_slice_in_dim(grad_down, weight_grad(hidden_last), columns, 0)
    grad_down = lax.dynamic_update_slice_in_dim(grad_down, weight_grad(hidden_first), 0, 0)
    return grad_gate, grad_up, grad_down


def solution(mesh):
    in_specs = (P("dp", "tensor"), P("dp", "tensor"), P("dp", "tensor"), P("tensor", "dp"))
    out_specs = (P("dp", "tensor"), P("dp", "tensor"), P("tensor", "dp"))
    return jax.shard_map(shards, mesh=mesh, in_specs=in_specs, out_specs=out_specs, check_vma=False)
```

```python
import jax
import jax.numpy as jnp
from jax import lax
from jax.sharding import PartitionSpec as P

WIRE = jnp.float16
WIRE_SCALE = 16.0


def after(value, *others):
    return lax.optimization_barrier((value,) + others)[0]


def together(*values):
    return list(lax.optimization_barrier(values))


def shards(cotangent, gate_pre, up_pre, down_weight):
    dp, tensor = lax.axis_size("dp"), lax.axis_size("tensor")
    line = dp // 2
    tokens, features = cotangent.shape
    hidden_units, half = down_weight.shape
    assert features == 2 * half and line == tensor and line % 2 == 0
    position, side = lax.axis_index("dp") // 2, lax.axis_index("dp") % 2
    shard = lax.axis_index("tensor")
    columns = hidden_units * 4 // 7

    def along(name, value, step, first, last):
        pairs = [(2 * at + s, 2 * (at + step) + s) for at in range(first, last + 1) for s in (0, 1)]
        with jax.named_scope(name):
            return lax.ppermute(value, "dp", pairs)

    def across(name, value):
        with jax.named_scope(name):
            return lax.ppermute(value, "dp", [(at, at ^ 1) for at in range(dp)])

    gate_vals = gate_pre.astype(jnp.float32)
    up_vals = up_pre.astype(jnp.float32)
    sigma = jax.nn.sigmoid(gate_vals)
    act_vals = gate_vals * sigma
    hidden = (act_vals * up_vals).astype(jnp.bfloat16)
    first, last = hidden[:, :columns], hidden[:, columns:]
    weight_first, weight_last = down_weight[:columns], down_weight[columns:]

    middle = columns // 4
    weight_other = [across("weight_side", weight_first[:middle])]

    share = 2 * tokens // tensor
    arrived = []
    for turn in range(tensor // 2):
        piece = lax.dynamic_slice_in_dim(cotangent, (position + 2 * turn) % tensor // 2 * share, share, 0)
        pairs = [
            ((2 * at + s) * tensor + owner, (2 * owner + s) * tensor + (at + 2 * turn) % tensor)
            for at in range(line)
            for s in (0, 1)
            for owner in range(tensor)
        ]
        with jax.named_scope("cotangent_spread"):
            arrived.append(lax.ppermute(piece, ("dp", "tensor"), pairs))
    odd = (position - shard) % 2
    turned = ((shard - position + odd) % line) // 2
    row = lax.dynamic_slice_in_dim(jnp.stack(arrived + arrived), turned, line // 2, 0)
    mine = jnp.where(side == 0, row[..., :half], row[..., half:])
    other = jnp.where(side == 0, row[..., half:], row[..., :half])

    last_other = across("hidden_last_side", last)
    first_sent = after(first, *arrived)
    first_up = along("hidden_first_up1", first_sent, 1, 0, line - 2)
    first_down = along("hidden_first_down1", first_sent, -1, 1, line - 1)
    theirs = across("cotangent_side", after(other, last_other))
    first_up, first_down = together(first_up, first_down)

    both_last = jnp.stack([last, last_other])
    last_up = along("hidden_last_up1", both_last, 1, 0, line - 2)
    last_down = along("hidden_last_down1", both_last, -1, 1, line - 1)
    bounds = [columns // 4, columns // 2, columns]
    weight_other.append(across("weight_side", after(weight_first[bounds[0] : bounds[1]], theirs)))
    weight_other.append(across("weight_side", after(weight_first[bounds[1] :], weight_other[1])))
    last_up, last_down = together(last_up, last_down)

    own = after(jnp.stack([mine, other, theirs])[:, :, None], weight_other[0])
    bit = tensor // 2
    while bit > 1:
        with jax.named_scope("cotangent_shares"):
            swapped = lax.ppermute(own, "tensor", [(at, at ^ bit) for at in range(tensor)])
        low = (shard // bit) % 2 == 0
        own = jnp.stack([jnp.where(low, own, swapped), jnp.where(low, swapped, own)], axis=3)
        own = own.reshape(3, line // 2, -1, share, half)
        bit //= 2
    own = after(own, first_up, weight_other[1])
    with jax.named_scope("cotangent_core"):
        swapped = lax.ppermute(own, "tensor", [(at, at ^ 1) for at in range(tensor)])
    whole = jnp.stack([jnp.where(odd == 0, own, swapped), jnp.where(odd == 0, swapped, own)], axis=2)
    mine, other, theirs = whole.reshape(3, line, tokens, half)
    features_of_all = jnp.stack([mine, theirs], axis=1)

    def product(left, right):
        return jnp.einsum("...f,hf->...h", left, right, preferred_element_type=jnp.float32)

    parts = {"last": product(features_of_all, weight_last) * WIRE_SCALE}

    weight_other = jnp.concatenate(weight_other)
    parts["first"] = (product(mine, weight_first) + product(other, weight_other)) * WIRE_SCALE

    rising = {"first": [first, first_up], "last": [both_last, last_up]}
    falling = {"first": [first, first_down], "last": [both_last, last_down]}

    def gather_step(which, step, *waits):
        up = along(f"hidden_{which}_up{step}", after(rising[which][-1], *waits), 1, step - 1, line - 2)
        down = along(f"hidden_{which}_down{step}", after(falling[which][-1], *waits), -1, 1, line - step)
        up, down = together(up, down)
        rising[which].append(up)
        falling[which].append(down)

    gather_step("first", 2)

    sums, arrived = {"last": (0.0, 0.0), "first": (0.0, 0.0)}, {}
    before, sent = {}, {}

    def sum_step(which, step, *waits):
        up, down = sums[which]
        message = sent[which] = after((parts[which][step] + up).astype(WIRE), *waits)
        up = along(f"dhid_{which}_up{step}", message, 1, 0, step - 1)
        message = after((parts[which][line - step] + down).astype(WIRE), *waits)
        down = along(f"dhid_{which}_down{step}", message, -1, line - step, line - 1)
        up, down = together(up, down)
        before[which], arrived[which] = arrived.get(which), up
        sums[which] = up.astype(jnp.float32), down.astype(jnp.float32)

    sum_step("last", 1)
    for step in range(2, line):
        if step > 2:
            gather_step("first", step, sent["last"])
        gather_step("last", step, sent["last"])

    def gathered(which, k):
        if k == 0:
            return rising[which][0]
        return jnp.where(position >= k, rising[which][k], falling[which][line - k])

    blocks = jnp.stack([gathered("first", k) for k in range(line)])
    exchanged = across("hidden_first_side", after(blocks, weight_other))

    for step in range(2, line):
        if step < line - 1:
            sum_step("last", step, weight_other, rising["first"][step])
            sum_step("first", step - 1, rising["first"][step])
        else:
            sum_step("last", step, rising["first"][step], rising["last"][step - 1])
            sum_step("first", step - 1, rising["first"][step], before["last"])
            exchanged = after(exchanged, arrived["last"])
            sum_step("first", step, rising["last"][step], arrived["last"], exchanged)

    pair = parts["last"][0] + sums["last"][0] + sums["last"][1]
    up, down, from_side = together(*sums["first"], across("dhid_last_side", pair[1].astype(WIRE)))
    dhid = [parts["first"][0] + up + down, pair[0] + from_side.astype(jnp.float32)]
    dhid = jnp.concatenate(dhid, axis=1) * (1.0 / WIRE_SCALE)

    grad_up = (dhid * act_vals).astype(jnp.bfloat16)
    grad_gate = (dhid * up_vals * sigma * (1.0 + gate_vals * (1.0 - sigma))).astype(jnp.bfloat16)

    hidden_first = jnp.stack([blocks, exchanged], axis=1)
    hidden_last = jnp.stack([gathered("last", k) for k in range(line)])

    def weight_grad(values):
        summed = jnp.einsum("kstc,kstf->cf", values, features_of_all, preferred_element_type=jnp.float32)
        return summed * (tokens * dp) ** (-0.5)

    grad_down = jnp.concatenate([weight_grad(hidden_first), weight_grad(hidden_last)])
    return grad_gate, grad_up, grad_down


def solution(mesh):
    in_specs = (P("dp", "tensor"), P("dp", "tensor"), P("dp", "tensor"), P("tensor", "dp"))
    out_specs = (P("dp", "tensor"), P("dp", "tensor"), P("tensor", "dp"))
    return jax.shard_map(shards, mesh=mesh, in_specs=in_specs, out_specs=out_specs, check_vma=False)
```

```python
import jax
import jax.numpy as jnp
from jax import lax
from jax.sharding import PartitionSpec as P

WIRE = jnp.float16
WIRE_SCALE = 16.0


def after(value, *others):
    return lax.optimization_barrier((value,) + others)[0]


def together(*values):
    return list(lax.optimization_barrier(values))


def shards(cotangent, gate_pre, up_pre, down_weight):
    dp, tensor = lax.axis_size("dp"), lax.axis_size("tensor")
    line = dp // 2
    tokens, features = cotangent.shape
    hidden_units, half = down_weight.shape
    assert features == 2 * half and line == tensor and line % 2 == 0
    position, side = lax.axis_index("dp") // 2, lax.axis_index("dp") % 2
    shard = lax.axis_index("tensor")
    columns = hidden_units * 4 // 7

    def along(name, value, step, first, last):
        pairs = [(2 * at + s, 2 * (at + step) + s) for at in range(first, last + 1) for s in (0, 1)]
        with jax.named_scope(name):
            return lax.ppermute(value, "dp", pairs)

    def across(name, value):
        with jax.named_scope(name):
            return lax.ppermute(value, "dp", [(at, at ^ 1) for at in range(dp)])

    gate_vals = gate_pre.astype(jnp.float32)
    up_vals = up_pre.astype(jnp.float32)
    sigma = jax.nn.sigmoid(gate_vals)
    act_vals = gate_vals * sigma
    hidden = (act_vals * up_vals).astype(jnp.bfloat16)
    first, last = hidden[:, :columns], hidden[:, columns:]
    weight_first, weight_last = down_weight[:columns], down_weight[columns:]

    middle = columns // 4
    weight_other = [across("weight_side", weight_first[:middle])]

    share = 2 * tokens // tensor
    arrived = []
    for turn in range(tensor // 2):
        piece = lax.dynamic_slice_in_dim(cotangent, (position + 2 * turn) % tensor // 2 * share, share, 0)
        pairs = [
            ((2 * at + s) * tensor + owner, (2 * owner + s) * tensor + (at + 2 * turn) % tensor)
            for at in range(line)
            for s in (0, 1)
            for owner in range(tensor)
        ]
        with jax.named_scope("cotangent_spread"):
            arrived.append(lax.ppermute(piece, ("dp", "tensor"), pairs))
    odd = (position - shard) % 2
    turned = ((shard - position + odd) % line) // 2
    row = lax.dynamic_slice_in_dim(jnp.stack(arrived + arrived), turned, line // 2, 0)
    mine = jnp.where(side == 0, row[..., :half], row[..., half:])
    other = jnp.where(side == 0, row[..., half:], row[..., :half])

    last_other = across("hidden_last_side", last)
    first_sent = after(first, *arrived)
    first_up = along("hidden_first_up1", first_sent, 1, 0, line - 2)
    first_down = along("hidden_first_down1", first_sent, -1, 1, line - 1)
    theirs = across("cotangent_side", after(other, last_other))
    first_up, first_down = together(first_up, first_down)

    both_last = jnp.stack([last, last_other])
    last_up = along("hidden_last_up1", both_last, 1, 0, line - 2)
    last_down = along("hidden_last_down1", both_last, -1, 1, line - 1)
    bounds = [columns // 4, columns // 2, columns]
    weight_other.append(across("weight_side", after(weight_first[bounds[0] : bounds[1]], theirs)))
    weight_other.append(across("weight_side", after(weight_first[bounds[1] :], weight_other[1])))
    last_up, last_down = together(last_up, last_down)

    own = after(jnp.stack([mine, other, theirs])[:, :, None], weight_other[0])
    bit = tensor // 2
    while bit > 1:
        with jax.named_scope("cotangent_shares"):
            swapped = lax.ppermute(own, "tensor", [(at, at ^ bit) for at in range(tensor)])
        low = (shard // bit) % 2 == 0
        own = jnp.stack([jnp.where(low, own, swapped), jnp.where(low, swapped, own)], axis=3)
        own = own.reshape(3, line // 2, -1, share, half)
        bit //= 2
    own = after(own, first_up, weight_other[1])
    with jax.named_scope("cotangent_core"):
        swapped = lax.ppermute(own, "tensor", [(at, at ^ 1) for at in range(tensor)])
    whole = jnp.stack([jnp.where(odd == 0, own, swapped), jnp.where(odd == 0, swapped, own)], axis=2)
    mine, other, theirs = whole.reshape(3, line, tokens, half)
    features_of_all = jnp.stack([mine, theirs], axis=1)

    def product(left, right):
        return jnp.einsum("...f,hf->...h", left, right, preferred_element_type=jnp.float32)

    parts = {"last": product(features_of_all, weight_last) * WIRE_SCALE}

    weight_other = jnp.concatenate(weight_other)
    parts["first"] = (product(mine, weight_first) + product(other, weight_other)) * WIRE_SCALE

    rising = {"first": [first, first_up], "last": [both_last, last_up]}
    falling = {"first": [first, first_down], "last": [both_last, last_down]}

    def gather_step(which, step, *waits):
        up = along(f"hidden_{which}_up{step}", after(rising[which][-1], *waits), 1, step - 1, line - 2)
        down = along(f"hidden_{which}_down{step}", after(falling[which][-1], *waits), -1, 1, line - step)
        rising[which].append(up)
        falling[which].append(down)

    gather_step("first", 2)

    sums, arrived = {"last": (0.0, 0.0), "first": (0.0, 0.0)}, {}
    before, sent = {}, {}

    def sum_step(which, step, *waits):
        up, down = sums[which]
        message = sent[which] = after((parts[which][step] + up).astype(WIRE), *waits)
        up = along(f"dhid_{which}_up{step}", message, 1, 0, step - 1)
        message = after((parts[which][line - step] + down).astype(WIRE), *waits)
        down = along(f"dhid_{which}_down{step}", message, -1, line - step, line - 1)
        up, down = together(up, down)
        before[which], arrived[which] = arrived.get(which), up
        sums[which] = up.astype(jnp.float32), down.astype(jnp.float32)

    sum_step("last", 1)
    rising["first"][2], falling["first"][2], _ = together(rising["first"][2], falling["first"][2], sent["last"])
    gather_step("first", 3, sent["last"])
    gather_step("last", 2, sent["last"])

    def gathered(which, k):
        if k == 0:
            return rising[which][0]
        return jnp.where(position >= k, rising[which][k], falling[which][line - k])

    def settle(which, step):
        up, down, _ = together(rising[which][step], falling[which][step], sent["last"])
        rising[which][step], falling[which][step] = up, down

    for step in range(2, line):
        if step < line - 1:
            sum_step("last", step, weight_other, rising["first"][step])
            settle("first", step + 1)
            settle("last", step)
            if step + 2 < line:
                gather_step("first", step + 2)
            else:
                blocks = jnp.stack([gathered("first", k) for k in range(line)])
                exchanged = across("hidden_first_side", after(blocks, weight_other))
            gather_step("last", step + 1)
            sum_step("first", step - 1, rising["first"][step])
        else:
            sum_step("last", step)
            settle("last", step)
            sum_step("first", step - 1, before["last"])
            exchanged = after(exchanged, arrived["last"])
            sum_step("first", step, rising["last"][step], arrived["last"], exchanged)

    pair = parts["last"][0] + sums["last"][0] + sums["last"][1]
    up, down, from_side = together(*sums["first"], across("dhid_last_side", pair[1].astype(WIRE)))
    dhid = [parts["first"][0] + up + down, pair[0] + from_side.astype(jnp.float32)]
    dhid = jnp.concatenate(dhid, axis=1) * (1.0 / WIRE_SCALE)

    grad_up = (dhid * act_vals).astype(jnp.bfloat16)
    grad_gate = (dhid * up_vals * sigma * (1.0 + gate_vals * (1.0 - sigma))).astype(jnp.bfloat16)

    hidden_first = jnp.stack([blocks, exchanged], axis=1)
    hidden_last = jnp.stack([gathered("last", k) for k in range(line)])

    def weight_grad(values):
        summed = jnp.einsum("kstc,kstf->cf", values, features_of_all, preferred_element_type=jnp.float32)
        return summed * (tokens * dp) ** (-0.5)

    grad_down = jnp.concatenate([weight_grad(hidden_first), weight_grad(hidden_last)])
    return grad_gate, grad_up, grad_down


def solution(mesh):
    in_specs = (P("dp", "tensor"), P("dp", "tensor"), P("dp", "tensor"), P("tensor", "dp"))
    out_specs = (P("dp", "tensor"), P("dp", "tensor"), P("tensor", "dp"))
    return jax.shard_map(shards, mesh=mesh, in_specs=in_specs, out_specs=out_specs, check_vma=False)
```

```python
import jax
import jax.numpy as jnp
from jax import lax
from jax.sharding import PartitionSpec as P

WIRE = jnp.float16
WIRE_SCALE = 16.0


def after(value, *others):
    return lax.optimization_barrier((value,) + others)[0]


def together(*values):
    return list(lax.optimization_barrier(values))


def shards(cotangent, gate_pre, up_pre, down_weight):
    dp, tensor = lax.axis_size("dp"), lax.axis_size("tensor")
    line = dp // 2
    tokens, features = cotangent.shape
    hidden_units, half = down_weight.shape
    assert features == 2 * half and line == tensor and line % 2 == 0
    position, side = lax.axis_index("dp") // 2, lax.axis_index("dp") % 2
    shard = lax.axis_index("tensor")
    columns = hidden_units * 4 // 7

    def along(name, value, step, first, last):
        pairs = [(2 * at + s, 2 * (at + step) + s) for at in range(first, last + 1) for s in (0, 1)]
        with jax.named_scope(name):
            return lax.ppermute(value, "dp", pairs)

    def across(name, value):
        with jax.named_scope(name):
            return lax.ppermute(value, "dp", [(at, at ^ 1) for at in range(dp)])

    gate_vals = gate_pre.astype(jnp.float32)
    up_vals = up_pre.astype(jnp.float32)
    sigma = jax.nn.sigmoid(gate_vals)
    act_vals = gate_vals * sigma
    hidden = (act_vals * up_vals).astype(jnp.bfloat16)
    first, last = hidden[:, :columns], hidden[:, columns:]
    weight_first, weight_last = down_weight[:columns], down_weight[columns:]

    middle = columns // 4
    weight_other = [across("weight_side", weight_first[:middle])]

    share = 2 * tokens // tensor
    arrived = []
    for turn in range(tensor // 2):
        piece = lax.dynamic_slice_in_dim(cotangent, (position + 2 * turn) % tensor // 2 * share, share, 0)
        pairs = [
            ((2 * at + s) * tensor + owner, (2 * owner + s) * tensor + (at + 2 * turn) % tensor)
            for at in range(line)
            for s in (0, 1)
            for owner in range(tensor)
        ]
        with jax.named_scope("cotangent_spread"):
            arrived.append(lax.ppermute(piece, ("dp", "tensor"), pairs))
    odd = (position - shard) % 2
    turned = ((shard - position + odd) % line) // 2
    row = lax.dynamic_slice_in_dim(jnp.stack(arrived + arrived), turned, line // 2, 0)
    mine = jnp.where(side == 0, row[..., :half], row[..., half:])
    other = jnp.where(side == 0, row[..., half:], row[..., :half])

    last_other = across("hidden_last_side", last)
    first_sent = after(first, *arrived)
    first_up = along("hidden_first_up1", first_sent, 1, 0, line - 2)
    first_down = along("hidden_first_down1", first_sent, -1, 1, line - 1)
    theirs = across("cotangent_side", after(other, last_other))
    first_up, first_down = together(first_up, first_down)

    both_last = jnp.stack([last, last_other])
    last_up = along("hidden_last_up1", both_last, 1, 0, line - 2)
    last_down = along("hidden_last_down1", both_last, -1, 1, line - 1)
    bounds = [columns // 4, columns // 2, columns]
    weight_other.append(across("weight_side", after(weight_first[bounds[0] : bounds[1]], theirs)))
    weight_other.append(across("weight_side", after(weight_first[bounds[1] :], weight_other[1])))
    last_up, last_down = together(last_up, last_down)

    own = after(jnp.stack([mine, other, theirs])[:, :, None], weight_other[0])
    bit = tensor // 2
    while bit > 1:
        with jax.named_scope("cotangent_shares"):
            swapped = lax.ppermute(own, "tensor", [(at, at ^ bit) for at in range(tensor)])
        low = (shard // bit) % 2 == 0
        own = jnp.stack([jnp.where(low, own, swapped), jnp.where(low, swapped, own)], axis=3)
        own = own.reshape(3, line // 2, -1, share, half)
        bit //= 2
    own = after(own, first_up, weight_other[1])
    with jax.named_scope("cotangent_core"):
        swapped = lax.ppermute(own, "tensor", [(at, at ^ 1) for at in range(tensor)])
    whole = jnp.stack([jnp.where(odd == 0, own, swapped), jnp.where(odd == 0, swapped, own)], axis=2)
    mine, other, theirs = whole.reshape(3, line, tokens, half)
    features_of_all = jnp.stack([mine, theirs], axis=1)

    def product(left, right):
        return jnp.einsum("...f,hf->...h", left, right, preferred_element_type=jnp.float32)

    parts = {"last": product(features_of_all, weight_last) * WIRE_SCALE}

    weight_other = jnp.concatenate(weight_other)
    parts["first"] = (product(mine, weight_first) + product(other, weight_other)) * WIRE_SCALE

    rising = {"first": [first, first_up], "last": [both_last, last_up]}
    falling = {"first": [first, first_down], "last": [both_last, last_down]}

    def gather_step(which, step, *waits):
        up = along(f"hidden_{which}_up{step}", after(rising[which][-1], *waits), 1, step - 1, line - 2)
        down = along(f"hidden_{which}_down{step}", after(falling[which][-1], *waits), -1, 1, line - step)
        rising[which].append(up)
        falling[which].append(down)

    gather_step("first", 2)

    sums, arrived = {"last": (0.0, 0.0), "first": (0.0, 0.0)}, {}
    before, sent, ended = {}, {}, {}

    def sum_step(which, step, *waits):
        up, down = sums[which]
        message = sent[which] = after((parts[which][step] + up).astype(WIRE), *waits)
        up = along(f"dhid_{which}_up{step}", message, 1, 0, step - 1)
        message = after((parts[which][line - step] + down).astype(WIRE), *waits)
        down = along(f"dhid_{which}_down{step}", message, -1, line - step, line - 1)
        if which == "last" or step < line - 1:
            up, down = together(up, down)
        before[which], arrived[which] = arrived.get(which), up
        ended[which] = up, down
        sums[which] = up.astype(jnp.float32), down.astype(jnp.float32)

    sum_step("last", 1)
    rising["first"][2], falling["first"][2], _ = together(rising["first"][2], falling["first"][2], sent["last"])
    gather_step("first", 3, sent["last"])
    gather_step("last", 2, sent["last"])

    def gathered(which, k):
        if k == 0:
            return rising[which][0]
        return jnp.where(position >= k, rising[which][k], falling[which][line - k])

    def settle(which, step, message):
        up, down, _ = together(rising[which][step], falling[which][step], message)
        rising[which][step], falling[which][step] = up, down

    for step in range(2, line):
        if step < line - 1:
            sum_step("last", step, weight_other, rising["first"][step])
            settle("first", step + 1, sent["last"])
            settle("last", step, sent["last"])
            if step + 2 < line:
                gather_step("first", step + 2)
            else:
                blocks = jnp.stack([gathered("first", k) for k in range(line)])
                exchanged = across("hidden_first_side", after(blocks, weight_other))
            gather_step("last", step + 1)
            sum_step("first", step - 1, rising["first"][step])
        else:
            sum_step("last", step)
            sum_step("first", step - 1, before["last"])
            settle("last", step, sent["first"])
            exchanged = after(exchanged, arrived["last"])
            sum_step("first", step, rising["last"][step], arrived["last"])

    hidden_first = jnp.stack([blocks, exchanged], axis=1)
    hidden_last = jnp.stack([gathered("last", k) for k in range(line)])

    def weight_grad(values):
        summed = jnp.einsum("kstc,kstf->cf", values, features_of_all, preferred_element_type=jnp.float32)
        return summed * (tokens * dp) ** (-0.5)

    grad_down = jnp.concatenate([weight_grad(hidden_first), weight_grad(hidden_last)])
    pair = parts["last"][0] + sums["last"][0] + sums["last"][1]
    from_side = across("dhid_last_side", pair[1].astype(WIRE))
    up, down, from_side, grad_down = together(*ended["first"], from_side, grad_down)
    dhid = [parts["first"][0] + up + down, pair[0] + from_side.astype(jnp.float32)]
    dhid = jnp.concatenate(dhid, axis=1) * (1.0 / WIRE_SCALE)

    grad_up = (dhid * act_vals).astype(jnp.bfloat16)
    grad_gate = (dhid * up_vals * sigma * (1.0 + gate_vals * (1.0 - sigma))).astype(jnp.bfloat16)
    return grad_gate, grad_up, grad_down


def solution(mesh):
    in_specs = (P("dp", "tensor"), P("dp", "tensor"), P("dp", "tensor"), P("tensor", "dp"))
    out_specs = (P("dp", "tensor"), P("dp", "tensor"), P("tensor", "dp"))
    return jax.shard_map(shards, mesh=mesh, in_specs=in_specs, out_specs=out_specs, check_vma=False)
```

```python
import jax
import jax.numpy as jnp
from jax import lax
from jax.sharding import PartitionSpec as P

WIRE = jnp.float16
WIRE_SCALE = 16.0


def after(value, *others):
    return lax.optimization_barrier((value,) + others)[0]


def together(*values):
    return list(lax.optimization_barrier(values))


def shards(cotangent, gate_pre, up_pre, down_weight):
    dp, tensor = lax.axis_size("dp"), lax.axis_size("tensor")
    line = dp // 2
    tokens, features = cotangent.shape
    hidden_units, half = down_weight.shape
    assert features == 2 * half and line == tensor and line % 2 == 0
    position, side = lax.axis_index("dp") // 2, lax.axis_index("dp") % 2
    shard = lax.axis_index("tensor")
    columns = hidden_units * 4 // 7

    def along(name, value, step, first, last):
        pairs = [(2 * at + s, 2 * (at + step) + s) for at in range(first, last + 1) for s in (0, 1)]
        with jax.named_scope(name):
            return lax.ppermute(value, "dp", pairs)

    def across(name, value):
        with jax.named_scope(name):
            return lax.ppermute(value, "dp", [(at, at ^ 1) for at in range(dp)])

    gate_vals = gate_pre.astype(jnp.float32)
    up_vals = up_pre.astype(jnp.float32)
    sigma = jax.nn.sigmoid(gate_vals)
    act_vals = gate_vals * sigma
    hidden = (act_vals * up_vals).astype(jnp.bfloat16)
    first, last = hidden[:, :columns], hidden[:, columns:]
    weight_first, weight_last = down_weight[:columns], down_weight[columns:]

    middle = columns // 4
    weight_other = [across("weight_side", weight_first[:middle])]

    share = 2 * tokens // tensor
    arrived = []
    for turn in range(tensor // 2):
        piece = lax.dynamic_slice_in_dim(cotangent, (position + 2 * turn) % tensor // 2 * share, share, 0)
        pairs = [
            ((2 * at + s) * tensor + owner, (2 * owner + s) * tensor + (at + 2 * turn) % tensor)
            for at in range(line)
            for s in (0, 1)
            for owner in range(tensor)
        ]
        with jax.named_scope("cotangent_spread"):
            arrived.append(lax.ppermute(piece, ("dp", "tensor"), pairs))
    odd = (position - shard) % 2
    turned = ((shard - position + odd) % line) // 2
    row = lax.dynamic_slice_in_dim(jnp.stack(arrived + arrived), turned, line // 2, 0)
    mine = jnp.where(side == 0, row[..., :half], row[..., half:])
    other = jnp.where(side == 0, row[..., half:], row[..., :half])

    last_other = across("hidden_last_side", last)
    first_sent = after(first, *arrived)
    first_up = along("hidden_first_up1", first_sent, 1, 0, line - 2)
    first_down = along("hidden_first_down1", first_sent, -1, 1, line - 1)
    theirs = across("cotangent_side", after(other, last_other))
    first_up, first_down = together(first_up, first_down)

    both_last = jnp.stack([last, last_other])
    last_up = along("hidden_last_up1", both_last, 1, 0, line - 2)
    last_down = along("hidden_last_down1", both_last, -1, 1, line - 1)
    bounds = [columns // 4, columns // 2, columns]
    weight_other.append(across("weight_side", after(weight_first[bounds[0] : bounds[1]], theirs)))
    weight_other.append(across("weight_side", after(weight_first[bounds[1] :], weight_other[1])))
    last_up, last_down = together(last_up, last_down)

    own = after(jnp.stack([mine, other, theirs])[:, :, None], weight_other[0], both_last)
    bit = tensor // 2
    while bit > 1:
        with jax.named_scope("cotangent_shares"):
            swapped = lax.ppermute(own, "tensor", [(at, at ^ bit) for at in range(tensor)])
        low = (shard // bit) % 2 == 0
        own = jnp.stack([jnp.where(low, own, swapped), jnp.where(low, swapped, own)], axis=3)
        own = own.reshape(3, line // 2, -1, share, half)
        bit //= 2
    own = after(own, first_up, weight_other[1])
    with jax.named_scope("cotangent_core"):
        swapped = lax.ppermute(own, "tensor", [(at, at ^ 1) for at in range(tensor)])
    whole = jnp.stack([jnp.where(odd == 0, own, swapped), jnp.where(odd == 0, swapped, own)], axis=2)
    mine, other, theirs = whole.reshape(3, line, tokens, half)
    features_of_all = jnp.stack([mine, theirs], axis=1)

    def product(left, right):
        return jnp.einsum("...f,hf->...h", left, right, preferred_element_type=jnp.float32)

    parts = {"last": product(features_of_all, weight_last) * WIRE_SCALE}

    weight_other = jnp.concatenate(weight_other)
    parts["first"] = (product(mine, weight_first) + product(other, weight_other)) * WIRE_SCALE

    rising = {"first": [first, first_up], "last": [both_last, last_up]}
    falling = {"first": [first, first_down], "last": [both_last, last_down]}

    def gather_step(which, step, *waits):
        up = along(f"hidden_{which}_up{step}", after(rising[which][-1], *waits), 1, step - 1, line - 2)
        down = along(f"hidden_{which}_down{step}", after(falling[which][-1], *waits), -1, 1, line - step)
        rising[which].append(up)
        falling[which].append(down)

    gather_step("first", 2)

    sums, arrived = {"last": (0.0, 0.0), "first": (0.0, 0.0)}, {}
    before, sent, ended = {}, {}, {}

    def sum_step(which, step, *waits):
        up, down = sums[which]
        message = sent[which] = after((parts[which][step] + up).astype(WIRE), *waits)
        up = along(f"dhid_{which}_up{step}", message, 1, 0, step - 1)
        message = after((parts[which][line - step] + down).astype(WIRE), *waits)
        down = along(f"dhid_{which}_down{step}", message, -1, line - step, line - 1)
        if which == "last" or step < line - 1:
            up, down = together(up, down)
        before[which], arrived[which] = arrived.get(which), up
        ended[which] = up, down
        sums[which] = up.astype(jnp.float32), down.astype(jnp.float32)

    sum_step("last", 1)
    rising["first"][2], falling["first"][2], _ = together(rising["first"][2], falling["first"][2], sent["last"])
    gather_step("first", 3, sent["last"])
    gather_step("last", 2, sent["last"])

    def gathered(which, k):
        if k == 0:
            return rising[which][0]
        return jnp.where(position >= k, rising[which][k], falling[which][line - k])

    def settle(which, step, message):
        up, down, _ = together(rising[which][step], falling[which][step], message)
        rising[which][step], falling[which][step] = up, down

    for step in range(2, line):
        if step < line - 1:
            sum_step("last", step, weight_other, rising["first"][step])
            settle("first", step + 1, sent["last"])
            settle("last", step, sent["last"])
            if step + 2 < line:
                gather_step("first", step + 2)
            else:
                blocks = jnp.stack([gathered("first", k) for k in range(line)])
                exchanged = across("hidden_first_side", after(blocks, weight_other))
            gather_step("last", step + 1)
            sum_step("first", step - 1, rising["first"][step])
        else:
            sum_step("last", step)
            sum_step("first", step - 1, before["last"])
            settle("last", step, sent["first"])
            exchanged = after(exchanged, arrived["last"])
            sum_step("first", step, rising["last"][step], arrived["last"])

    hidden_first = jnp.stack([blocks, exchanged], axis=1)
    hidden_last = jnp.stack([gathered("last", k) for k in range(line)])

    def weight_grad(values):
        summed = jnp.einsum("kstc,kstf->cf", values, features_of_all, preferred_element_type=jnp.float32)
        return summed * (tokens * dp) ** (-0.5)

    grad_down = jnp.concatenate([weight_grad(hidden_first), weight_grad(hidden_last)])
    pair = parts["last"][0] + sums["last"][0] + sums["last"][1]
    from_side = across("dhid_last_side", pair[1].astype(WIRE))
    up, down, from_side, grad_down = together(*ended["first"], from_side, grad_down)
    dhid = [parts["first"][0] + up + down, pair[0] + from_side.astype(jnp.float32)]
    dhid = jnp.concatenate(dhid, axis=1) * (1.0 / WIRE_SCALE)

    grad_up = (dhid * act_vals).astype(jnp.bfloat16)
    grad_gate = (dhid * up_vals * sigma * (1.0 + gate_vals * (1.0 - sigma))).astype(jnp.bfloat16)
    return grad_gate, grad_up, grad_down


def solution(mesh):
    in_specs = (P("dp", "tensor"), P("dp", "tensor"), P("dp", "tensor"), P("tensor", "dp"))
    out_specs = (P("dp", "tensor"), P("dp", "tensor"), P("tensor", "dp"))
    return jax.shard_map(shards, mesh=mesh, in_specs=in_specs, out_specs=out_specs, check_vma=False)
```

```python
import jax
import jax.numpy as jnp
from jax import lax
from jax.sharding import PartitionSpec as P

WIRE = jnp.float16
WIRE_SCALE = 32.0


def after(value, *others):
    return lax.optimization_barrier((value,) + others)[0]


def together(*values):
    return list(lax.optimization_barrier(values))


def shards(cotangent, gate_pre, up_pre, down_weight):
    dp, tensor = lax.axis_size("dp"), lax.axis_size("tensor")
    line = dp // 2
    tokens, features = cotangent.shape
    hidden_units, half = down_weight.shape
    assert features == 2 * half and line == tensor and line % 2 == 0
    position, side = lax.axis_index("dp") // 2, lax.axis_index("dp") % 2
    shard = lax.axis_index("tensor")
    columns = hidden_units * 4 // 7

    def along(name, value, step, first, last):
        pairs = [(2 * at + s, 2 * (at + step) + s) for at in range(first, last + 1) for s in (0, 1)]
        with jax.named_scope(name):
            return lax.ppermute(value, "dp", pairs)

    def across(name, value):
        with jax.named_scope(name):
            return lax.ppermute(value, "dp", [(at, at ^ 1) for at in range(dp)])

    gate_vals = gate_pre.astype(jnp.float32)
    up_vals = up_pre.astype(jnp.float32)
    sigma = jax.nn.sigmoid(gate_vals)
    act_vals = gate_vals * sigma
    hidden = (act_vals * up_vals).astype(jnp.bfloat16)
    first, last = hidden[:, :columns], hidden[:, columns:]
    weight_first, weight_last = down_weight[:columns], down_weight[columns:]

    middle = columns // 4
    weight_other = [across("weight_side", weight_first[:middle])]

    share = 2 * tokens // tensor
    arrived = []
    for turn in range(tensor // 2):
        piece = lax.dynamic_slice_in_dim(cotangent, (position + 2 * turn) % tensor // 2 * share, share, 0)
        pairs = [
            ((2 * at + s) * tensor + owner, (2 * owner + s) * tensor + (at + 2 * turn) % tensor)
            for at in range(line)
            for s in (0, 1)
            for owner in range(tensor)
        ]
        with jax.named_scope("cotangent_spread"):
            arrived.append(lax.ppermute(piece, ("dp", "tensor"), pairs))
    odd = (position - shard) % 2
    turned = ((shard - position + odd) % line) // 2
    row = lax.dynamic_slice_in_dim(jnp.stack(arrived + arrived), turned, line // 2, 0)
    mine = jnp.where(side == 0, row[..., :half], row[..., half:])
    other = jnp.where(side == 0, row[..., half:], row[..., :half])

    last_other = across("hidden_last_side", last)
    first_sent = after(first, *arrived)
    first_up = along("hidden_first_up1", first_sent, 1, 0, line - 2)
    first_down = along("hidden_first_down1", first_sent, -1, 1, line - 1)
    theirs = across("cotangent_side", after(other, last_other))
    first_up, first_down = together(first_up, first_down)

    both_last = jnp.stack([last, last_other])
    last_up = along("hidden_last_up1", both_last, 1, 0, line - 2)
    last_down = along("hidden_last_down1", both_last, -1, 1, line - 1)
    bounds = [columns // 4, columns // 2, columns]
    weight_other.append(across("weight_side", after(weight_first[bounds[0] : bounds[1]], theirs)))
    weight_other.append(across("weight_side", after(weight_first[bounds[1] :], weight_other[1])))
    last_up, last_down = together(last_up, last_down)

    own = after(jnp.stack([mine, other, theirs])[:, :, None], weight_other[0])
    bit = tensor // 2
    while bit > 1:
        with jax.named_scope("cotangent_shares"):
            swapped = lax.ppermute(own, "tensor", [(at, at ^ bit) for at in range(tensor)])
        low = (shard // bit) % 2 == 0
        own = jnp.stack([jnp.where(low, own, swapped), jnp.where(low, swapped, own)], axis=3)
        own = own.reshape(3, line // 2, -1, share, half)
        bit //= 2
    own = after(own, first_up, weight_other[1])
    with jax.named_scope("cotangent_core"):
        swapped = lax.ppermute(own, "tensor", [(at, at ^ 1) for at in range(tensor)])
    whole = jnp.stack([jnp.where(odd == 0, own, swapped), jnp.where(odd == 0, swapped, own)], axis=2)
    mine, other, theirs = whole.reshape(3, line, tokens, half)
    features_of_all = jnp.stack([mine, theirs], axis=1)

    def product(left, right):
        return jnp.einsum("...f,hf->...h", left, right, preferred_element_type=jnp.float32)

    parts = {"last": product(features_of_all, weight_last) * WIRE_SCALE}

    weight_other = jnp.concatenate(weight_other)
    parts["first"] = (product(mine, weight_first) + product(other, weight_other)) * WIRE_SCALE

    rising = {"first": [first, first_up], "last": [both_last, last_up]}
    falling = {"first": [first, first_down], "last": [both_last, last_down]}

    def gather_step(which, step, *waits):
        up = along(f"hidden_{which}_up{step}", after(rising[which][-1], *waits), 1, step - 1, line - 2)
        down = along(f"hidden_{which}_down{step}", after(falling[which][-1], *waits), -1, 1, line - step)
        rising[which].append(up)
        falling[which].append(down)

    gather_step("first", 2)

    sums, arrived = {"last": (0.0, 0.0), "first": (0.0, 0.0)}, {}
    before, sent, ended = {}, {}, {}

    def sum_step(which, step, *waits):
        up, down = sums[which]
        message = sent[which] = after((parts[which][step] + up).astype(WIRE), *waits)
        up = along(f"dhid_{which}_up{step}", message, 1, 0, step - 1)
        message = after((parts[which][line - step] + down).astype(WIRE), *waits)
        down = along(f"dhid_{which}_down{step}", message, -1, line - step, line - 1)
        if which == "last" or step < line - 1:
            up, down = together(up, down)
        before[which], arrived[which] = arrived.get(which), up
        ended[which] = up, down
        sums[which] = up.astype(jnp.float32), down.astype(jnp.float32)

    sum_step("last", 1)
    rising["first"][2], falling["first"][2], _ = together(rising["first"][2], falling["first"][2], sent["last"])
    gather_step("first", 3, sent["last"])
    gather_step("last", 2, sent["last"])

    def gathered(which, k):
        if k == 0:
            return rising[which][0]
        return jnp.where(position >= k, rising[which][k], falling[which][line - k])

    def settle(which, step, message):
        up, down, _ = together(rising[which][step], falling[which][step], message)
        rising[which][step], falling[which][step] = up, down

    for step in range(2, line):
        if step < line - 1:
            sum_step("last", step, weight_other, rising["first"][step])
            settle("first", step + 1, sent["last"])
            settle("last", step, sent["last"])
            if step + 2 < line:
                gather_step("first", step + 2)
            else:
                blocks = jnp.stack([gathered("first", k) for k in range(line)])
                exchanged = across("hidden_first_side", after(blocks, weight_other))
            gather_step("last", step + 1)
            sum_step("first", step - 1, rising["first"][step])
        else:
            sum_step("last", step)
            sum_step("first", step - 1, before["last"])
            settle("last", step, sent["first"])
            exchanged = after(exchanged, arrived["last"])
            sum_step("first", step, rising["last"][step], arrived["last"])

    hidden_first = jnp.stack([blocks, exchanged], axis=1)
    hidden_last = jnp.stack([gathered("last", k) for k in range(line)])

    def weight_grad(values):
        summed = jnp.einsum("kstc,kstf->cf", values, features_of_all, preferred_element_type=jnp.float32)
        return summed * (tokens * dp) ** (-0.5)

    grad_down = jnp.concatenate([weight_grad(hidden_first), weight_grad(hidden_last)])
    pair = parts["last"][0] + sums["last"][0] + sums["last"][1]
    from_side = across("dhid_last_side", pair[1].astype(WIRE))
    up, down, from_side, grad_down = together(*ended["first"], from_side, grad_down)
    dhid = [parts["first"][0] + up + down, pair[0] + from_side.astype(jnp.float32)]
    dhid = jnp.concatenate(dhid, axis=1) * (1.0 / WIRE_SCALE)

    grad_up = (dhid * act_vals).astype(jnp.bfloat16)
    grad_gate = (dhid * up_vals * sigma * (1.0 + gate_vals * (1.0 - sigma))).astype(jnp.bfloat16)
    return grad_gate, grad_up, grad_down


def solution(mesh):
    in_specs = (P("dp", "tensor"), P("dp", "tensor"), P("dp", "tensor"), P("tensor", "dp"))
    out_specs = (P("dp", "tensor"), P("dp", "tensor"), P("tensor", "dp"))
    return jax.shard_map(shards, mesh=mesh, in_specs=in_specs, out_specs=out_specs, check_vma=False)
```
